32 devices in a mesh: groups: 2 (over y), dev: 4 (over z), sub: 4 (over x, core).
Axes of the slice: x: 2, y: 2, z: 4, core: 2. Of those that a mesh axis runs over, the one named last changes fastest.
Arguments:
- query_pre: bfloat16 [8, 16, 256, 128], P('dev', ('groups', 'sub')), parts along dimension 1, may hold values from -0.5390625 to 0.5390625
- key_pre: bfloat16 [8, 16, 256, 128], P('dev', ('groups', 'sub')), parts along dimension 1, may hold values from -0.375 to 0.375
- value_pre: bfloat16 [8, 16, 256, 128], P('dev', ('groups', 'sub')), parts along dimension 1, may hold values from -6 to 6
- decay_pre: float32 [8, 16, 256], P('dev', ('groups', 'sub')), parts along dimension 1, may hold values from -0.75 to 0
- blocks: int32 [16], P('groups'), parts along dimension 0, may hold values from 1 to 2, as said below
- dest_map: int32 [16], P('groups'), parts along dimension 0, may hold values from 0 to 3, as said below
- query_dec: bfloat16 [16, 4, 128, 8], P(('groups', 'dev'), None, 'sub'), parts along dimension 0, may hold values from -0.5390625 to 0.5390625
- key_dec: bfloat16 [16, 4, 128, 8], P(('groups', 'dev'), None, 'sub'), parts along dimension 0, may hold values from -0.375 to 0.375
- value_dec: bfloat16 [16, 4, 8, 128], P(('groups', 'dev')), parts along dimension 0, may hold values from -6 to 6
- decay_dec: float32 [16, 4, 8], P(('groups', 'dev')), parts along dimension 0, may hold values from -0.75 to 0
- gate_dec: bfloat16 [16, 4, 1024], P(('groups', 'dev'), None, 'sub'), parts along dimension 0, may hold values from -6 to 6
- norm_gain: float32 [1024], P('sub'), may hold values from 0.1 to 1.9
Outputs:
- prefill_out: bfloat16 [8, 16, 256, 128], P('dev', ('groups', 'sub')), parts along dimension 1
- decode_out: bfloat16 [16, 4, 1024], P(('groups', 'dev'), None, 'sub'), parts along dimension 0
- final_state: float32 [16, 8, 128, 128], P(('groups', 'dev'), None, 'sub'), parts along dimension 0
The draws below stay inside these ranges and needn't reach their ends.
There are 2 independent parts, one for each index of `groups`. The reference program is written for one: setup_inputs(seed, part) draws one part's arguments, and reference() takes and returns one part's arrays. A program takes and returns all parts, laid end to end along the dimension named above; an argument that names none is the same for every part. Nothing has to cross between parts.
Inputs may be any that keep to these rules, and one draw needn't show every extreme that they name: At least one request has 2 blocks. `dest_map`: every value is named by exactly 2 requests, and the 2 requests of one aligned block of ids name distinct values.
All inputs are finite; a program needn't handle non-finite values.
Results may differ from the reference program's by a relative error of at most 0.001.
Values sent between devices are 32-bit elements; how exact they have to be, the bound alone decides.
A program may use at most 128 MiB of HBM per device.

```python
import math
import jax
import jax.numpy as jnp
from jax import lax

HDIM = 128
HEADS = 8
D = 1024
REQUEST_COUNT = 8
BLOCK_POSITIONS = 128
MAX_PROMPT_BLOCKS = 2
DECODE_STEPS = 4
N_DEV = 4
N_SUB = 4


def head_rates(key):
    base = jax.random.fold_in(key, 11)
    selector = jax.random.uniform(jax.random.fold_in(base, 1), (HEADS,))
    fast_share = 0.5
    chain_length = MAX_PROMPT_BLOCKS * BLOCK_POSITIONS + DECODE_STEPS
    fast_rates = jnp.exp(jax.random.uniform(jax.random.fold_in(base, 2), (HEADS,), minval=math.log(0.02), maxval=math.log(0.035)))
    slow_rates = jnp.exp(jax.random.uniform(jax.random.fold_in(base, 3), (HEADS,), minval=math.log(0.1 / chain_length), maxval=math.log(1.0 / chain_length)))
    return jnp.where(selector < fast_share, fast_rates, slow_rates)


def draw_decay_pre(key, part):
    decay_rates = head_rates(key)
    prompt_length = MAX_PROMPT_BLOCKS * BLOCK_POSITIONS
    random_offset = jax.random.uniform(jax.random.fold_in(key, 41), (HEADS, REQUEST_COUNT, prompt_length), minval=0.5, maxval=1.5)
    spike_mask = jax.random.uniform(jax.random.fold_in(key, 42), (REQUEST_COUNT, prompt_length)) < 2.0 / prompt_length
    retained_fraction = jax.random.uniform(jax.random.fold_in(key, 43), (REQUEST_COUNT, prompt_length), minval=0.5, maxval=0.8)
    spike_draws = jnp.where(spike_mask, jnp.log(retained_fraction), 0.0)
    return (-decay_rates[:, None, None] * random_offset + spike_draws[None]).astype(jnp.float32)


def draw_decay_dec(key, part):
    decay_rates = head_rates(key)
    random_offset = jax.random.uniform(jax.random.fold_in(key, 51), (REQUEST_COUNT, DECODE_STEPS, HEADS), minval=0.5, maxval=1.5)
    spike_mask = jax.random.uniform(jax.random.fold_in(key, 52), (REQUEST_COUNT, DECODE_STEPS)) < 2.0 / (MAX_PROMPT_BLOCKS * BLOCK_POSITIONS + DECODE_STEPS)
    retained_fraction = jax.random.uniform(jax.random.fold_in(key, 53), (REQUEST_COUNT, DECODE_STEPS), minval=0.5, maxval=0.8)
    spike_draws = jnp.where(spike_mask, jnp.log(retained_fraction), 0.0)
    return (-decay_rates[None, None, :] * random_offset + spike_draws[..., None]).astype(jnp.float32)


def draw_blocks(key, part):
    counts = jax.random.randint(jax.random.fold_in(key, 21), (REQUEST_COUNT,), 1, MAX_PROMPT_BLOCKS + 1)
    chosen_index = jax.random.randint(jax.random.fold_in(key, 22), (), 0, REQUEST_COUNT)
    return counts.at[chosen_index].set(MAX_PROMPT_BLOCKS).astype(jnp.int32)


def group_permutation(group_key):
    return jax.random.permutation(group_key, REQUEST_COUNT // N_SUB)


def draw_dest_map(key, part):
    group_size = REQUEST_COUNT // N_SUB
    device_order = jax.random.permutation(jax.random.fold_in(key, 31), N_DEV)
    group_keys = jax.random.split(jax.random.fold_in(key, 32), N_SUB)
    inner_order = jax.vmap(group_permutation)(group_keys)
    positions = (jnp.arange(N_SUB, dtype=jnp.int32)[:, None] * group_size + inner_order) % N_DEV
    return device_order[positions.reshape(-1)].astype(jnp.int32)


def level_of(key, shape, cuts, smallest, top_value):
    level = 1.0
    for position, shards_of in cuts:
        steps = jax.random.uniform(jax.random.fold_in(jax.random.fold_in(key, 6), position), (shards_of,), jnp.float32, smallest / len(cuts), top_value / len(cuts))
        level = level * jnp.repeat(jnp.exp(steps), shape[position] // shards_of).reshape((-1,) + (1,) * (len(shape) - 1 - position))
    return level


def normal_values(rng, extent, scale, most, cuts=(), held_as=jnp.bfloat16):
    values = jax.random.normal(rng, extent, jnp.float32) * scale
    if len(cuts) > 0:
        values = level_of(rng, extent, cuts, -0.22, 0.18) * values
    return jnp.clip(values, min=-most, max=most).astype(held_as)


def setup_inputs(seed: int = 0, part: int = 0) -> dict:
    splits = jax.random.split(jax.random.key(seed), 13)
    part_splits = jax.random.split(jax.random.fold_in(splits[12], part), 13)
    return {
        "query_pre": normal_values(part_splits[0], (HEADS, REQUEST_COUNT, MAX_PROMPT_BLOCKS * BLOCK_POSITIONS, HDIM), 0.09, 0.5390625, ((0, 4), (1, 4))),
        "key_pre": normal_values(part_splits[1], (HEADS, REQUEST_COUNT, MAX_PROMPT_BLOCKS * BLOCK_POSITIONS, HDIM), 0.0625, 0.375, ((0, 4), (1, 4))),
        "value_pre": normal_values(part_splits[2], (HEADS, REQUEST_COUNT, MAX_PROMPT_BLOCKS * BLOCK_POSITIONS, HDIM), 1.0, 6.0, ((0, 4), (1, 4))),
        "decay_pre": draw_decay_pre(jax.random.fold_in(jax.random.fold_in(splits[12], part), 71), part),
        "blocks": draw_blocks(jax.random.fold_in(jax.random.fold_in(splits[12], part), 71), part),
        "dest_map": draw_dest_map(jax.random.fold_in(jax.random.fold_in(splits[12], part), 71), part),
        "query_dec": normal_values(part_splits[6], (REQUEST_COUNT, DECODE_STEPS, HDIM, HEADS), 0.09, 0.5390625, ((0, 4), (2, 4))),
        "key_dec": normal_values(part_splits[7], (REQUEST_COUNT, DECODE_STEPS, HDIM, HEADS), 0.0625, 0.375, ((0, 4), (2, 4))),
        "value_dec": normal_values(part_splits[8], (REQUEST_COUNT, DECODE_STEPS, HEADS, HDIM), 1.0, 6.0, ((0, 4),)),
        "decay_dec": draw_decay_dec(jax.random.fold_in(jax.random.fold_in(splits[12], part), 71), part),
        "gate_dec": normal_values(part_splits[10], (REQUEST_COUNT, DECODE_STEPS, D), 1.0, 6.0, ((0, 4), (2, 4))),
        "norm_gain": jnp.clip(1.0 + 0.18 * jax.random.normal(splits[11], (D,), jnp.float32), 0.1, 1.9),
    }


HIGHEST = lax.Precision.HIGHEST
EPSILON = 1e-06

def prefill_blocks(query_input, key_input, value_input, log_decay, block_count):
    positions = jnp.arange(query_input.shape[2], dtype=jnp.int32)
    valid_mask = (positions[None, :] < block_count[:, None] * BLOCK_POSITIONS).astype(jnp.float32)
    log_decay = log_decay * valid_mask[None]
    key_input = key_input * valid_mask.astype(jnp.bfloat16)[None, :, :, None]
    within = positions[:BLOCK_POSITIONS]
    causal_mask = within[:, None] >= within[None, :]
    head_size = query_input.shape[3]
    carried = jnp.zeros(query_input.shape[:2] + (head_size, head_size), jnp.float32)
    pieces = []
    for block_index in range(MAX_PROMPT_BLOCKS):
        block_start = block_index * BLOCK_POSITIONS
        query_block = query_input[:, :, block_start:block_start + BLOCK_POSITIONS].astype(jnp.float32)
        key_block = key_input[:, :, block_start:block_start + BLOCK_POSITIONS].astype(jnp.float32)
        value_block = value_input[:, :, block_start:block_start + BLOCK_POSITIONS].astype(jnp.float32)
        cumulative = jnp.cumsum(log_decay[:, :, block_start:block_start + BLOCK_POSITIONS], axis=-1)
        offsets = jnp.where(causal_mask, cumulative[..., :, None] - cumulative[..., None, :], 0.0)
        weights = jnp.where(causal_mask, jnp.exp(offsets), 0.0)
        scores = jnp.einsum('hgtd,hgud->hgtu', query_block, key_block, precision=HIGHEST) * weights
        inner_part = jnp.einsum('hgtu,hgud->hgtd', scores, value_block, precision=HIGHEST)
        outer_part = jnp.exp(cumulative)[..., None] * jnp.einsum('hgtd,hgde->hgte', query_block, carried, precision=HIGHEST)
        pieces.append(((inner_part + outer_part) * valid_mask[None, :, block_start:block_start + BLOCK_POSITIONS, None]).astype(jnp.bfloat16))
        tail_decay = jnp.exp(cumulative[..., -1:] - cumulative)
        carried = jnp.exp(cumulative[..., -1])[..., None, None] * carried + jnp.einsum('hgtd,hgte->hgde', key_block * tail_decay[..., None], value_block, precision=HIGHEST)
    return (jnp.concatenate(pieces, axis=2), carried)

def advance(carried_state, inputs):
    query_step, key_step, value_step, decay_step = inputs
    key_cols = jnp.swapaxes(key_step.astype(jnp.float32), 1, 2)
    carried_state = jnp.exp(decay_step)[..., None, None] * carried_state + key_cols[..., None] * value_step.astype(jnp.float32)[:, :, None, :]
    reading = jnp.einsum('jhc,jhcd->jhd', jnp.swapaxes(query_step.astype(jnp.float32), 1, 2), carried_state, precision=HIGHEST)
    return (carried_state, reading)

def reference(query_pre, key_pre, value_pre, decay_pre, blocks, dest_map, query_dec, key_dec, value_dec, decay_dec, gate_dec, norm_gain):

    def one_head(inputs):
        query_input, key_input, value_input, log_decay = inputs
        outputs, carried = prefill_blocks(query_input[None], key_input[None], value_input[None], log_decay[None], blocks)
        return (outputs[0], carried[0])
    prefill_out, carried = lax.map(one_head, (query_pre, key_pre, value_pre, decay_pre))
    request_ids = jnp.arange(REQUEST_COUNT, dtype=jnp.int32)
    slot_order = jnp.argsort(dest_map * REQUEST_COUNT + request_ids).astype(jnp.int32)
    initial = jnp.transpose(jnp.take(carried, slot_order, axis=1), (1, 0, 2, 3))
    final_state, readings = lax.scan(advance, initial, (jnp.moveaxis(query_dec, 1, 0), jnp.moveaxis(key_dec, 1, 0), jnp.moveaxis(value_dec, 1, 0), jnp.moveaxis(decay_dec, 1, 0)))
    outputs_all = jnp.moveaxis(readings, 0, 1).reshape(REQUEST_COUNT, DECODE_STEPS, D)
    inverse_rms = lax.rsqrt(lax.optimization_barrier(jnp.mean(outputs_all * outputs_all, axis=-1)) + EPSILON)[..., None]
    decode_out = (outputs_all * inverse_rms * norm_gain * jax.nn.sigmoid(gate_dec.astype(jnp.float32))).astype(jnp.bfloat16)
    return (prefill_out, decode_out, final_state)
```

```python
import functools

import jax
import jax.numpy as jnp
from jax import lax
from jax.experimental import pallas as pl
from jax.experimental.pallas import tpu as pltpu
from jax.sharding import PartitionSpec as P

BLOCK = 128
EPSILON = 1e-06
HIGHEST = lax.Precision.HIGHEST
F32 = jnp.float32
BF16 = jnp.bfloat16
CHUNK = 8


def each(low, high, step):
    if high - low <= 8:
        for i in range(low, high):
            step(i)
    else:

        def turn(i, carry):
            step(i)
            return carry

        lax.fori_loop(low, high, turn, 0)


def dot(a, b, contract, precision=None):
    return lax.dot_general(
        a, b, (contract, ((), ())), precision=precision, preferred_element_type=F32
    )


NN = ((1,), (0,))
NT = ((1,), (1,))
TN = ((0,), (0,))


def split(x):
    high = x.astype(BF16)
    return high, (x - high.astype(F32)).astype(BF16)


def iota(shape, dimension):
    return lax.broadcasted_iota(jnp.int32, shape, dimension)


def kernel(
    n_dev,
    n_sub,
    q_ref,
    k_ref,
    v_ref,
    d_ref,
    blocks_ref,
    dest_ref,
    qd_ref,
    kd_ref,
    vd_ref,
    dd_ref,
    gate_ref,
    gain_ref,
    out_hbm,
    dec_ref,
    fin_hbm,
    sbuf,
    bbuf,
    rbuf,
    fsbuf,
    pbuf,
    dbuf,
    qbuf,
    ebuf,
    ybuf,
    ysum,
    send_a,
    recv_a,
    send_b,
    recv_b,
    send_y,
    recv_y,
    local,
    *mids,
):
    heads, group, length, width = q_ref.shape
    prompt_blocks = length // BLOCK
    slots, steps, rows, all_heads = qd_ref.shape
    requests = dest_ref.shape[0]
    chunks = all_heads // CHUNK
    lanes = CHUNK * rows
    sub = lax.axis_index("sub")
    dev = lax.axis_index("dev")

    barrier = pltpu.get_barrier_semaphore()

    def greet_sub(i):
        pl.semaphore_signal(
            barrier,
            inc=1,
            device_id={"sub": lax.rem(sub + i, n_sub)},
            device_id_type=pl.DeviceIdType.MESH,
        )

    def greet_dev(i):
        pl.semaphore_signal(
            barrier,
            inc=1,
            device_id={"dev": lax.rem(dev + i, n_dev)},
            device_id_type=pl.DeviceIdType.MESH,
        )

    each(1, n_sub, greet_sub)
    each(1, n_dev, greet_dev)

    lower = iota((BLOCK, BLOCK), 0) >= iota((BLOCK, BLOCK), 1)
    diagonal = iota((BLOCK, BLOCK), 0) == iota((BLOCK, BLOCK), 1)

    def live(g, b):
        return jnp.where(blocks_ref[sub * group + g] > b, 1.0, 0.0).astype(F32)

    def cumulative(hd, g, b):
        row = dbuf[hd, g, :, b * BLOCK : (b + 1) * BLOCK] * live(g, b)
        return jnp.sum(
            jnp.where(lower, jnp.broadcast_to(row, (BLOCK, BLOCK)), 0.0),
            axis=1,
            keepdims=True,
        )

    def state(hd, g):
        after = None
        weighted = []
        for b in reversed(range(prompt_blocks)):
            col = cumulative(hd, g, b)
            last = col[BLOCK - 1 :, :]
            tail = last - col if after is None else last - col + after
            after = last if after is None else after + last
            part = v_ref[hd, g, b * BLOCK : (b + 1) * BLOCK, :].astype(F32)
            weighted.append(part * (jnp.exp(tail) * live(g, b)))
        high, low = split(jnp.concatenate(weighted[::-1], axis=0))
        both = dot(k_ref[hd, g], jnp.concatenate([high, low], axis=1), TN)
        total = both[:, :width] + both[:, width:]
        for s in range(n_sub):
            sbuf[hd, s, g] = total[s * rows : (s + 1) * rows, :]

    def output(hd, g):
        cols = [cumulative(hd, g, b) for b in range(prompt_blocks)]
        flat = [
            jnp.sum(
                jnp.where(diagonal, jnp.broadcast_to(c, (BLOCK, BLOCK)), 0.0),
                axis=0,
                keepdims=True,
            )
            for c in cols
        ]
        for b in range(prompt_blocks):
            q = q_ref[hd, g, b * BLOCK : (b + 1) * BLOCK, :]
            total = None
            before = None
            for a in reversed(range(b + 1)):
                k = k_ref[hd, g, a * BLOCK : (a + 1) * BLOCK, :]
                v = v_ref[hd, g, a * BLOCK : (a + 1) * BLOCK, :]
                if a == b:
                    weights = jnp.where(
                        lower, jnp.exp(jnp.where(lower, cols[b] - flat[a], 0.0)), 0.0
                    )
                else:
                    gap = cols[a][BLOCK - 1 :, :] - flat[a]
                    if before is not None:
                        gap = gap + before
                    weights = jnp.exp(cols[b] + gap)
                    ending = cols[a][BLOCK - 1 :, :]
                    before = ending if before is None else before + ending
                high, low = split(dot(q, k, NT) * weights)
                term = dot(
                    jnp.concatenate([high, low], axis=1),
                    jnp.concatenate([v, v], axis=0),
                    NN,
                )
                total = term if total is None else total + term
            pbuf[hd, g, b * BLOCK : (b + 1) * BLOCK, :] = (total * live(g, b)).astype(
                BF16
            )

    def copy_a(hd, i):
        to = lax.rem(sub + i, n_sub)
        return pltpu.make_async_remote_copy(
            src_ref=sbuf.at[hd, to],
            dst_ref=mids[hd].at[pl.ds(sub * group, group)],
            send_sem=send_a.at[hd, i],
            recv_sem=recv_a.at[hd, i],
            device_id={"sub": to},
            device_id_type=pl.DeviceIdType.MESH,
        )

    def copy_b(hd, i):
        to = lax.rem(dev + i, n_dev)
        return pltpu.make_async_remote_copy(
            src_ref=bbuf.at[hd, i],
            dst_ref=rbuf.at[dev, hd],
            send_sem=send_b.at[hd, i],
            recv_sem=recv_b.at[hd, i],
            device_id={"dev": to},
            device_id_type=pl.DeviceIdType.MESH,
        )

    def copy_y(i):
        return pltpu.make_async_remote_copy(
            src_ref=ybuf.at[0],
            dst_ref=ybuf.at[i],
            send_sem=send_y.at[i],
            recv_sem=recv_y.at[i],
            device_id={"sub": lax.rem(sub + i, n_sub)},
            device_id_type=pl.DeviceIdType.MESH,
        )

    def owned(r):
        def look(n, found):
            first, second = found
            mine = dest_ref[n] == r
            return (
                jnp.where(mine, jnp.minimum(first, n), first),
                jnp.where(mine, jnp.maximum(second, n), second),
            )

        found = (jnp.int32(requests - 1), jnp.int32(0))
        if requests <= 8:
            for n in range(requests):
                found = look(n, found)
            return found
        return lax.fori_loop(0, requests, look, found)

    def decode_ahead(j, c):
        eight = iota((CHUNK, CHUNK), 0) == iota((CHUNK, CHUNK), 1)
        n = steps * CHUNK
        pieces = []
        total = jnp.zeros((1, CHUNK), F32)
        for s in range(steps):
            total = total + dd_ref[j, s : s + 1, c * CHUNK : (c + 1) * CHUNK]
            pieces.append(
                jnp.sum(
                    jnp.where(eight, jnp.broadcast_to(total, (CHUNK, CHUNK)), 0.0),
                    axis=1,
                    keepdims=True,
                )
            )
        col = jnp.concatenate(pieces, axis=0)
        square_row, square_col = iota((n, n), 0), iota((n, n), 1)
        row = jnp.sum(
            jnp.where(square_row == square_col, jnp.broadcast_to(col, (n, n)), 0.0),
            axis=0,
            keepdims=True,
        )
        seen = ((square_row & (CHUNK - 1)) == (square_col & (CHUNK - 1))) & (
            square_row >= square_col
        )
        weights = jnp.where(seen, jnp.exp(jnp.where(seen, col - row, 0.0)), 0.0)
        spread = (
            iota((rows, lanes), 0) == lax.rem(iota((rows, lanes), 1), rows)
        ).astype(BF16)
        own = iota((CHUNK, lanes), 0) == lax.div(iota((CHUNK, lanes), 1), rows)

        def diagonal_blocks(ref):
            return jnp.concatenate(
                [
                    jnp.where(
                        own,
                        dot(ref[j, s, :, c * CHUNK : (c + 1) * CHUNK], spread, TN),
                        0.0,
                    )
                    for s in range(steps)
                ],
                axis=0,
            )

        qb = diagonal_blocks(qd_ref).astype(BF16)
        kb = diagonal_blocks(kd_ref)
        vb = jnp.concatenate(
            [
                vd_ref[j, s, c * CHUNK : (c + 1) * CHUNK, :].astype(F32)
                for s in range(steps)
            ],
            axis=0,
        )
        mixed = dot(qb, kb.astype(BF16), NT) * weights
        ybuf[0, c, j] = dot(mixed, vb, NN, HIGHEST)
        tail = jnp.exp(jnp.concatenate([pieces[-1]] * steps, axis=0) - col)
        update = dot(kb * tail, vb, TN, HIGHEST)
        for h in range(CHUNK):
            fsbuf[j, c * CHUNK + h] = update[h * rows : (h + 1) * rows, :]
        qbuf[c, j] = qb
        ebuf[c, j] = jnp.broadcast_to(jnp.exp(col), (n, width))

    def decode(j, c):
        per = CHUNK // heads
        last = (steps - 1) * CHUNK
        parts = [
            rbuf[c * per + h // heads, h % heads, j] for h in range(CHUNK)
        ]
        high, low = split(jnp.concatenate(parts, axis=0))
        both = dot(qbuf[c, j], jnp.concatenate([high, low], axis=1), NN)
        ybuf[0, c, j] = (both[:, :width] + both[:, width:]) * ebuf[c, j] + ybuf[0, c, j]
        for h in range(CHUNK):
            fsbuf[j, c * CHUNK + h] = (
                parts[h] * ebuf[c, j, last + h : last + h + 1, :]
                + fsbuf[j, c * CHUNK + h]
            )

    for hd in range(heads):
        for g in range(group):
            dbuf[hd, g] = d_ref[hd, g : g + 1, :]
        each(0, group, functools.partial(state, hd))
        if hd == 0:
            pl.semaphore_wait(barrier, n_sub - 1 + n_dev - 1)
        each(1, n_sub, lambda i: copy_a(hd, i).start())
        mids[hd][pl.ds(sub * group, group)] = sbuf[hd, sub]

    for c in range(chunks):
        for j in range(slots):
            decode_ahead(j, c)

    def save(hd):
        return pltpu.make_async_copy(pbuf.at[hd], out_hbm.at[hd], local.at[hd])

    for hd in range(heads):
        each(1, n_sub, lambda i: copy_a(hd, i).wait_recv())

        def pass_on(i):
            first, second = owned(lax.rem(dev + i, n_dev))
            bbuf[hd, i, 0] = mids[hd][first]
            bbuf[hd, i, 1] = mids[hd][second]
            copy_b(hd, i).start()

        each(1, n_dev, pass_on)
        first, second = owned(dev)
        rbuf[dev, hd, 0] = mids[hd][first]
        rbuf[dev, hd, 1] = mids[hd][second]

    for hd in range(heads):
        each(0, group, functools.partial(output, hd))
        save(hd).start()

    for hd in range(heads):
        each(1, n_dev, lambda i: copy_b(hd, i).wait_recv())
    for c in range(chunks):
        for j in range(slots):
            decode(j, c)
    each(1, n_sub, lambda i: copy_y(i).start())
    final = pltpu.make_async_copy(fsbuf, fin_hbm, local.at[heads])
    final.start()
    share = all_heads // n_sub
    gates = [jax.nn.sigmoid(gate_ref[j].astype(F32)) * gain_ref[...] for j in range(slots)]
    each(1, n_sub, lambda i: copy_y(i).wait_recv())
    for j in range(slots):
        square = jnp.zeros((steps, width), F32)
        for c in range(chunks):
            y = ybuf[0, c, j]
            for i in range(1, n_sub):
                y = y + ybuf[i, c, j]
            for s in range(steps):
                ysum[j, s, c * CHUNK : (c + 1) * CHUNK, :] = y[
                    s * CHUNK : (s + 1) * CHUNK, :
                ]
            square = square + jnp.sum((y * y).reshape(steps, CHUNK, width), axis=1)
        mean = jnp.sum(square, axis=1, keepdims=True) / (all_heads * width)
        inverse = lax.rsqrt(mean + EPSILON)
        for h in range(share):
            y = jnp.concatenate(
                [ysum[j, s, pl.ds(sub * share + h, 1), :] for s in range(steps)], axis=0
            )
            gate = gates[j][:, h * width : (h + 1) * width]
            dec_ref[j, :, h * width : (h + 1) * width] = (y * inverse * gate).astype(
                BF16
            )
    for hd in range(heads):
        each(1, n_sub, lambda i: copy_a(hd, i).wait_send())
        each(1, n_dev, lambda i: copy_b(hd, i).wait_send())
        save(hd).wait()
    each(1, n_sub, lambda i: copy_y(i).wait_send())
    final.wait()


def body(n_dev, n_sub, *args):
    q, _, _, _, _, dest, qd = args[:7]
    heads, group, length, width = q.shape
    slots, steps, rows, all_heads = qd.shape
    requests = dest.shape[0]
    chunks = all_heads // CHUNK
    args = args[:11] + (args[11].reshape(1, -1),)
    vmem = pl.BlockSpec(memory_space=pltpu.VMEM)
    smem = pl.BlockSpec(memory_space=pltpu.SMEM)
    hbm = pl.BlockSpec(memory_space=pl.ANY)
    dma = pltpu.SemaphoreType.DMA
    return pl.pallas_call(
        functools.partial(kernel, n_dev, n_sub),
        out_shape=(
            jax.ShapeDtypeStruct(q.shape, BF16),
            jax.ShapeDtypeStruct(args[10].shape, BF16),
            jax.ShapeDtypeStruct((slots, all_heads, rows, width), F32),
        ),
        in_specs=[vmem] * 4 + [smem] * 2 + [vmem] * 6,
        out_specs=(hbm, vmem, hbm),
        scratch_shapes=[
            pltpu.VMEM((heads, n_sub, group, rows, width), F32),
            pltpu.VMEM((heads, n_dev, slots, rows, width), F32),
            pltpu.VMEM((n_dev, heads, slots, rows, width), F32),
            pltpu.VMEM((slots, all_heads, rows, width), F32),
            pltpu.VMEM(q.shape, BF16),
            pltpu.VMEM((heads, group, 1, length), F32),
            pltpu.VMEM((chunks, slots, steps * CHUNK, CHUNK * rows), BF16),
            pltpu.VMEM((chunks, slots, steps * CHUNK, width), F32),
            pltpu.VMEM((n_sub, chunks, slots, steps * CHUNK, width), F32),
            pltpu.VMEM((slots, steps, all_heads, width), F32),
            dma((heads, n_sub)),
            dma((heads, n_sub)),
            dma((heads, n_dev)),
            dma((heads, n_dev)),
            dma((n_sub,)),
            dma((n_sub,)),
            dma((heads + 1,)),
        ]
        + [pltpu.VMEM((requests, rows, width), F32)] * heads,
        compiler_params=pltpu.CompilerParams(
            collective_id=0, has_side_effects=True, vmem_limit_bytes=48 * 2**20
        ),
    )(*args)


def solution(mesh):
    placed = (
        P("dev", ("groups", "sub"), None, None),
        P("dev", ("groups", "sub"), None, None),
        P("dev", ("groups", "sub"), None, None),
        P("dev", ("groups", "sub"), None),
        P("groups"),
        P("groups"),
        P(("groups", "dev"), None, "sub", None),
        P(("groups", "dev"), None, "sub", None),
        P(("groups", "dev"), None, None, None),
        P(("groups", "dev"), None, None),
        P(("groups", "dev"), None, "sub"),
        P("sub"),
    )
    return jax.shard_map(
        functools.partial(body, mesh.shape["dev"], mesh.shape["sub"]),
        mesh=mesh,
        in_specs=placed,
        out_specs=(
            P("dev", ("groups", "sub"), None, None),
            P(("groups", "dev"), None, "sub"),
            P(("groups", "dev"), None, "sub", None),
        ),
        check_vma=False,
    )
```

```python
import functools

import jax
import jax.numpy as jnp
from jax import lax
from jax.experimental import pallas as pl
from jax.experimental.pallas import tpu as pltpu
from jax.sharding import PartitionSpec as P

BLOCK = 128
EPSILON = 1e-06
HIGHEST = lax.Precision.HIGHEST
F32 = jnp.float32
BF16 = jnp.bfloat16
CHUNK = 8


def each(low, high, step):
    if high - low <= 8:
        for i in range(low, high):
            step(i)
    else:

        def turn(i, carry):
            step(i)
            return carry

        lax.fori_loop(low, high, turn, 0)


def dot(a, b, contract, precision=None):
    return lax.dot_general(
        a, b, (contract, ((), ())), precision=precision, preferred_element_type=F32
    )


NN = ((1,), (0,))
NT = ((1,), (1,))
TN = ((0,), (0,))


def split(x):
    high = x.astype(BF16)
    return high, (x - high.astype(F32)).astype(BF16)


def iota(shape, dimension):
    return lax.broadcasted_iota(jnp.int32, shape, dimension)


def kernel(
    n_dev,
    n_sub,
    q_hbm,
    k_hbm,
    v_hbm,
    d_hbm,
    blocks_ref,
    dest_ref,
    qd_hbm,
    kd_hbm,
    vd_hbm,
    dd_hbm,
    pbuf,
    fsbuf,
    ybuf,
    q_ref,
    k_ref,
    v_ref,
    d_ref,
    qd_ref,
    kd_ref,
    vd_ref,
    dd_ref,
    sbuf,
    bbuf,
    rbuf,
    dbuf,
    qbuf,
    ebuf,
    send_a,
    recv_a,
    send_b,
    recv_b,
    send_y,
    recv_y,
    local,
    *mids,
):
    heads, group, length, width = q_ref.shape
    prompt_blocks = length // BLOCK
    slots, steps, all_heads, rows = qd_ref.shape
    requests = dest_ref.shape[0]
    chunks = all_heads // CHUNK
    lanes = CHUNK * rows
    sub = lax.axis_index("sub")
    dev = lax.axis_index("dev")

    loads = [
        pltpu.make_async_copy(source, target, local.at[i])
        for i, (source, target) in enumerate(
            (
                (d_hbm, d_ref),
                (v_hbm, v_ref),
                (k_hbm, k_ref),
                (q_hbm, q_ref),
                (dd_hbm, dd_ref),
                (kd_hbm, kd_ref),
                (qd_hbm, qd_ref),
                (vd_hbm, vd_ref),
            )
        )
    ]
    for load in loads:
        load.start()
    barrier = pltpu.get_barrier_semaphore()

    def greet_sub(i):
        pl.semaphore_signal(
            barrier,
            inc=1,
            device_id={"sub": lax.rem(sub + i, n_sub)},
            device_id_type=pl.DeviceIdType.MESH,
        )

    def greet_dev(i):
        pl.semaphore_signal(
            barrier,
            inc=1,
            device_id={"dev": lax.rem(dev + i, n_dev)},
            device_id_type=pl.DeviceIdType.MESH,
        )

    each(1, n_sub, greet_sub)
    each(1, n_dev, greet_dev)

    lower = iota((BLOCK, BLOCK), 0) >= iota((BLOCK, BLOCK), 1)
    diagonal = iota((BLOCK, BLOCK), 0) == iota((BLOCK, BLOCK), 1)

    def live(g, b):
        return jnp.where(blocks_ref[sub * group + g] > b, 1.0, 0.0).astype(F32)

    def cumulative(hd, g, b):
        row = dbuf[hd, g, :, b * BLOCK : (b + 1) * BLOCK] * live(g, b)
        return jnp.sum(
            jnp.where(lower, jnp.broadcast_to(row, (BLOCK, BLOCK)), 0.0),
            axis=1,
            keepdims=True,
        )

    def state(hd, g):
        after = None
        weighted = []
        for b in reversed(range(prompt_blocks)):
            col = cumulative(hd, g, b)
            last = col[BLOCK - 1 :, :]
            tail = last - col if after is None else last - col + after
            after = last if after is None else after + last
            part = v_ref[hd, g, b * BLOCK : (b + 1) * BLOCK, :].astype(F32)
            weighted.append(part * (jnp.exp(tail) * live(g, b)))
        high, low = split(jnp.concatenate(weighted[::-1], axis=0))
        both = dot(k_ref[hd, g], jnp.concatenate([high, low], axis=1), TN)
        total = both[:, :width] + both[:, width:]
        for s in range(n_sub):
            sbuf[hd, s, g] = total[s * rows : (s + 1) * rows, :]

    def output(hd, g):
        cols = [cumulative(hd, g, b) for b in range(prompt_blocks)]
        flat = [
            jnp.sum(
                jnp.where(diagonal, jnp.broadcast_to(c, (BLOCK, BLOCK)), 0.0),
                axis=0,
                keepdims=True,
            )
            for c in cols
        ]
        for b in range(prompt_blocks):
            q = q_ref[hd, g, b * BLOCK : (b + 1) * BLOCK, :]
            total = None
            before = None
            for a in reversed(range(b + 1)):
                k = k_ref[hd, g, a * BLOCK : (a + 1) * BLOCK, :]
                v = v_ref[hd, g, a * BLOCK : (a + 1) * BLOCK, :]
                if a == b:
                    weights = jnp.where(
                        lower, jnp.exp(jnp.where(lower, cols[b] - flat[a], 0.0)), 0.0
                    )
                else:
                    gap = cols[a][BLOCK - 1 :, :] - flat[a]
                    if before is not None:
                        gap = gap + before
                    weights = jnp.exp(cols[b] + gap)
                    ending = cols[a][BLOCK - 1 :, :]
                    before = ending if before is None else before + ending
                high, low = split(dot(q, k, NT) * weights)
                term = dot(
                    jnp.concatenate([high, low], axis=1),
                    jnp.concatenate([v, v], axis=0),
                    NN,
                )
                total = term if total is None else total + term
            pbuf[hd, g, b * BLOCK : (b + 1) * BLOCK, :] = (total * live(g, b)).astype(
                BF16
            )

    def copy_a(hd, i):
        to = lax.rem(sub + i, n_sub)
        return pltpu.make_async_remote_copy(
            src_ref=sbuf.at[hd, to],
            dst_ref=mids[hd].at[pl.ds(sub * group, group)],
            send_sem=send_a.at[hd, i],
            recv_sem=recv_a.at[hd, i],
            device_id={"sub": to},
            device_id_type=pl.DeviceIdType.MESH,
        )

    def copy_b(hd, i):
        to = lax.rem(dev + i, n_dev)
        return pltpu.make_async_remote_copy(
            src_ref=bbuf.at[hd, i],
            dst_ref=rbuf.at[dev, hd],
            send_sem=send_b.at[hd, i],
            recv_sem=recv_b.at[hd, i],
            device_id={"dev": to},
            device_id_type=pl.DeviceIdType.MESH,
        )

    def copy_y(i):
        return pltpu.make_async_remote_copy(
            src_ref=ybuf.at[0],
            dst_ref=ybuf.at[i],
            send_sem=send_y.at[i],
            recv_sem=recv_y.at[i],
            device_id={"sub": lax.rem(sub + i, n_sub)},
            device_id_type=pl.DeviceIdType.MESH,
        )

    def owned(r):
        def look(n, found):
            first, second = found
            mine = dest_ref[n] == r
            return (
                jnp.where(mine, jnp.minimum(first, n), first),
                jnp.where(mine, jnp.maximum(second, n), second),
            )

        found = (jnp.int32(requests - 1), jnp.int32(0))
        if requests <= 8:
            for n in range(requests):
                found = look(n, found)
            return found
        return lax.fori_loop(0, requests, look, found)

    def decode_ahead(j, c):
        eight = iota((CHUNK, CHUNK), 0) == iota((CHUNK, CHUNK), 1)
        n = steps * CHUNK
        pieces = []
        total = jnp.zeros((1, CHUNK), F32)
        for s in range(steps):
            total = total + dd_ref[j, s : s + 1, c * CHUNK : (c + 1) * CHUNK]
            pieces.append(
                jnp.sum(
                    jnp.where(eight, jnp.broadcast_to(total, (CHUNK, CHUNK)), 0.0),
                    axis=1,
                    keepdims=True,
                )
            )
        col = jnp.concatenate(pieces, axis=0)
        square_row, square_col = iota((n, n), 0), iota((n, n), 1)
        row = jnp.sum(
            jnp.where(square_row == square_col, jnp.broadcast_to(col, (n, n)), 0.0),
            axis=0,
            keepdims=True,
        )
        seen = ((square_row & (CHUNK - 1)) == (square_col & (CHUNK - 1))) & (
            square_row >= square_col
        )
        weights = jnp.where(seen, jnp.exp(jnp.where(seen, col - row, 0.0)), 0.0)
        spread = (
            iota((rows, lanes), 0) == lax.rem(iota((rows, lanes), 1), rows)
        ).astype(BF16)
        own = iota((CHUNK, lanes), 0) == lax.div(iota((CHUNK, lanes), 1), rows)

        def diagonal_blocks(ref):
            return jnp.concatenate(
                [
                    jnp.where(
                        own,
                        dot(ref[j, s, c * CHUNK : (c + 1) * CHUNK, :], spread, NN),
                        0.0,
                    )
                    for s in range(steps)
                ],
                axis=0,
            )

        qb = diagonal_blocks(qd_ref).astype(BF16)
        kb = diagonal_blocks(kd_ref)
        vb = jnp.concatenate(
            [
                vd_ref[j, s, c * CHUNK : (c + 1) * CHUNK, :].astype(F32)
                for s in range(steps)
            ],
            axis=0,
        )
        mixed = dot(qb, kb.astype(BF16), NT) * weights
        ybuf[0, c, j] = dot(mixed, vb, NN, HIGHEST)
        tail = jnp.exp(jnp.concatenate([pieces[-1]] * steps, axis=0) - col)
        update = dot(kb * tail, vb, TN, HIGHEST)
        for h in range(CHUNK):
            fsbuf[j, c * CHUNK + h] = update[h * rows : (h + 1) * rows, :]
        qbuf[c, j] = qb
        ebuf[c, j] = jnp.broadcast_to(jnp.exp(col), (n, width))

    def decode(j, c):
        per = CHUNK // heads
        last = (steps - 1) * CHUNK
        parts = [
            rbuf[c * per + h // heads, h % heads, j] for h in range(CHUNK)
        ]
        high, low = split(jnp.concatenate(parts, axis=0))
        both = dot(qbuf[c, j], jnp.concatenate([high, low], axis=1), NN)
        ybuf[0, c, j] = (both[:, :width] + both[:, width:]) * ebuf[c, j] + ybuf[0, c, j]
        for h in range(CHUNK):
            fsbuf[j, c * CHUNK + h] = (
                parts[h] * ebuf[c, j, last + h : last + h + 1, :]
                + fsbuf[j, c * CHUNK + h]
            )

    for load in loads[:3]:
        load.wait()
    for hd in range(heads):
        for g in range(group):
            dbuf[hd, g] = d_ref[hd, g : g + 1, :]
        each(0, group, functools.partial(state, hd))
        if hd == 0:
            pl.semaphore_wait(barrier, n_sub - 1 + n_dev - 1)
        each(1, n_sub, lambda i: copy_a(hd, i).start())
        mids[hd][pl.ds(sub * group, group)] = sbuf[hd, sub]
    for load in loads[3:]:
        load.wait()

    for hd in range(heads):
        each(1, n_sub, lambda i: copy_a(hd, i).wait_recv())

        def pass_on(i):
            first, second = owned(lax.rem(dev + i, n_dev))
            bbuf[hd, i, 0] = mids[hd][first]
            bbuf[hd, i, 1] = mids[hd][second]
            copy_b(hd, i).start()

        each(1, n_dev, pass_on)
        first, second = owned(dev)
        rbuf[dev, hd, 0] = mids[hd][first]
        rbuf[dev, hd, 1] = mids[hd][second]
        if hd + 1 < heads:
            each(0, group, functools.partial(output, hd))

    for c in range(chunks):
        for j in range(slots):
            decode_ahead(j, c)
    each(0, group, functools.partial(output, heads - 1))

    for hd in range(heads):
        each(1, n_dev, lambda i: copy_b(hd, i).wait_recv())
    for c in range(chunks):
        for j in range(slots):
            decode(j, c)
    each(1, n_sub, lambda i: copy_y(i).start())
    for hd in range(heads):
        each(1, n_sub, lambda i: copy_a(hd, i).wait_send())
        each(1, n_dev, lambda i: copy_b(hd, i).wait_send())
    each(1, n_sub, lambda i: copy_y(i).wait())


def finish(
    n_sub, out_ref, fin_ref, y_ref, gate_ref, gain_ref, out_hbm, dec_ref, fin_hbm, ysum, sems
):
    saves = [
        pltpu.make_async_copy(out_ref, out_hbm, sems.at[0]),
        pltpu.make_async_copy(fin_ref, fin_hbm, sems.at[1]),
    ]
    for save in saves:
        save.start()
    _, chunks, slots, _, width = y_ref.shape
    _, steps, all_heads, _ = ysum.shape
    sub = lax.axis_index("sub")
    share = all_heads // n_sub
    for j in range(slots):
        square = jnp.zeros((steps, width), F32)
        for c in range(chunks):
            y = y_ref[0, c, j]
            for i in range(1, n_sub):
                y = y + y_ref[i, c, j]
            for s in range(steps):
                ysum[j, s, c * CHUNK : (c + 1) * CHUNK, :] = y[
                    s * CHUNK : (s + 1) * CHUNK, :
                ]
            square = square + jnp.sum((y * y).reshape(steps, CHUNK, width), axis=1)
        mean = jnp.sum(square, axis=1, keepdims=True) / (all_heads * width)
        inverse = lax.rsqrt(mean + EPSILON)
        gates = jax.nn.sigmoid(gate_ref[j].astype(F32)) * gain_ref[...]
        for h in range(share):
            y = jnp.concatenate(
                [ysum[j, s, pl.ds(sub * share + h, 1), :] for s in range(steps)], axis=0
            )
            gate = gates[:, h * width : (h + 1) * width]
            dec_ref[j, :, h * width : (h + 1) * width] = (y * inverse * gate).astype(
                BF16
            )
    for save in saves:
        save.wait()


def body(n_dev, n_sub, *args):
    q, k, v, d, blocks, dest, qd, kd, vd, dd, gate, gain = args
    heads, group, length, width = q.shape
    slots, steps, rows, all_heads = qd.shape
    requests = dest.shape[0]
    chunks = all_heads // CHUNK
    vmem = pl.BlockSpec(memory_space=pltpu.VMEM)
    smem = pl.BlockSpec(memory_space=pltpu.SMEM)
    hbm = pl.BlockSpec(memory_space=pltpu.HBM)
    dma = pltpu.SemaphoreType.DMA
    turned = (slots, steps, all_heads, rows)
    state = jax.ShapeDtypeStruct((slots, all_heads, rows, width), F32)
    parts = (n_sub, chunks, slots, steps * CHUNK, width)
    made = pl.pallas_call(
        functools.partial(kernel, n_dev, n_sub),
        out_shape=(
            jax.ShapeDtypeStruct(q.shape, BF16),
            state,
            jax.ShapeDtypeStruct(parts, F32),
        ),
        in_specs=[hbm] * 4 + [smem] * 2 + [hbm] * 4,
        out_specs=(vmem, vmem, vmem),
        scratch_shapes=[
            pltpu.VMEM(q.shape, BF16),
            pltpu.VMEM(q.shape, BF16),
            pltpu.VMEM(q.shape, BF16),
            pltpu.VMEM(d.shape, F32),
            pltpu.VMEM(turned, BF16),
            pltpu.VMEM(turned, BF16),
            pltpu.VMEM(vd.shape, BF16),
            pltpu.VMEM(dd.shape, F32),
            pltpu.VMEM((heads, n_sub, group, rows, width), F32),
            pltpu.VMEM((heads, n_dev, slots, rows, width), F32),
            pltpu.VMEM((n_dev, heads, slots, rows, width), F32),
            pltpu.VMEM((heads, group, 1, length), F32),
            pltpu.VMEM((chunks, slots, steps * CHUNK, CHUNK * rows), BF16),
            pltpu.VMEM((chunks, slots, steps * CHUNK, width), F32),
            dma((heads, n_sub)),
            dma((heads, n_sub)),
            dma((heads, n_dev)),
            dma((heads, n_dev)),
            dma((n_sub,)),
            dma((n_sub,)),
            dma((8,)),
        ]
        + [pltpu.VMEM((requests, rows, width), F32)] * heads,
        compiler_params=pltpu.CompilerParams(
            collective_id=0, has_side_effects=True, vmem_limit_bytes=40 * 2**20
        ),
    )(
        q,
        k,
        v,
        d,
        blocks,
        dest,
        jnp.swapaxes(qd, 2, 3),
        jnp.swapaxes(kd, 2, 3),
        vd,
        dd,
    )
    out, fin, y = made
    out, dec, fin = pl.pallas_call(
        functools.partial(finish, n_sub),
        out_shape=(
            jax.ShapeDtypeStruct(q.shape, BF16),
            jax.ShapeDtypeStruct(gate.shape, BF16),
            state,
        ),
        in_specs=[pl.BlockSpec(memory_space=pl.ANY)] * 2 + [vmem] * 3,
        out_specs=(hbm, vmem, hbm),
        scratch_shapes=[pltpu.VMEM((slots, steps, all_heads, width), F32), dma((2,))],
        compiler_params=pltpu.CompilerParams(vmem_limit_bytes=16 * 2**20),
    )(out, fin, y, gate, gain.reshape(1, -1))
    return out, dec, fin


def solution(mesh):
    placed = (
        P("dev", ("groups", "sub"), None, None),
        P("dev", ("groups", "sub"), None, None),
        P("dev", ("groups", "sub"), None, None),
        P("dev", ("groups", "sub"), None),
        P("groups"),
        P("groups"),
        P(("groups", "dev"), None, "sub", None),
        P(("groups", "dev"), None, "sub", None),
        P(("groups", "dev"), None, None, None),
        P(("groups", "dev"), None, None),
        P(("groups", "dev"), None, "sub"),
        P("sub"),
    )
    return jax.shard_map(
        functools.partial(body, mesh.shape["dev"], mesh.shape["sub"]),
        mesh=mesh,
        in_specs=placed,
        out_specs=(
            P("dev", ("groups", "sub"), None, None),
            P(("groups", "dev"), None, "sub"),
            P(("groups", "dev"), None, "sub", None),
        ),
        check_vma=False,
    )
```

```python
import functools

import jax
import jax.numpy as jnp
from jax import lax
from jax.experimental import pallas as pl
from jax.experimental.pallas import tpu as pltpu
from jax.sharding import PartitionSpec as P

BLOCK = 128
EPSILON = 1e-06
HIGHEST = lax.Precision.HIGHEST
F32 = jnp.float32
BF16 = jnp.bfloat16
CHUNK = 8


def each(low, high, step):
    if high - low <= 8:
        for i in range(low, high):
            step(i)
    else:

        def turn(i, carry):
            step(i)
            return carry

        lax.fori_loop(low, high, turn, 0)


def dot(a, b, contract, precision=None):
    return lax.dot_general(
        a, b, (contract, ((), ())), precision=precision, preferred_element_type=F32
    )


NN = ((1,), (0,))
NT = ((1,), (1,))
TN = ((0,), (0,))


def split(x):
    high = x.astype(BF16)
    return high, (x - high.astype(F32)).astype(BF16)


def iota(shape, dimension):
    return lax.broadcasted_iota(jnp.int32, shape, dimension)


def kernel(
    n_dev,
    n_sub,
    q_hbm,
    k_hbm,
    v_hbm,
    d_hbm,
    blocks_ref,
    dest_ref,
    qd_hbm,
    kd_hbm,
    vd_hbm,
    dd_hbm,
    gate_hbm,
    gain_hbm,
    out_hbm,
    dec_ref,
    fin_hbm,
    pbuf,
    fsbuf,
    ybuf,
    ysum,
    gate_ref,
    gain_ref,
    q_ref,
    k_ref,
    v_ref,
    d_ref,
    qd_ref,
    kd_ref,
    vd_ref,
    dd_ref,
    sbuf,
    bbuf,
    rbuf,
    dbuf,
    qbuf,
    ebuf,
    send_a,
    recv_a,
    send_b,
    recv_b,
    send_y,
    recv_y,
    local,
    saved,
    *mids,
):
    heads, group, length, width = q_ref.shape
    prompt_blocks = length // BLOCK
    slots, steps, all_heads, rows = qd_ref.shape
    requests = dest_ref.shape[0]
    chunks = all_heads // CHUNK
    lanes = CHUNK * rows
    sub = lax.axis_index("sub")
    dev = lax.axis_index("dev")

    loads = [
        pltpu.make_async_copy(source, target, local.at[i])
        for i, (source, target) in enumerate(
            (
                (d_hbm, d_ref),
                (v_hbm, v_ref),
                (k_hbm, k_ref),
                (q_hbm, q_ref),
                (dd_hbm, dd_ref),
                (kd_hbm, kd_ref),
                (qd_hbm, qd_ref),
                (vd_hbm, vd_ref),
                (gate_hbm, gate_ref),
                (gain_hbm, gain_ref),
            )
        )
    ]
    for load in loads:
        load.start()
    barrier = pltpu.get_barrier_semaphore()

    def greet_sub(i):
        pl.semaphore_signal(
            barrier,
            inc=1,
            device_id={"sub": lax.rem(sub + i, n_sub)},
            device_id_type=pl.DeviceIdType.MESH,
        )

    def greet_dev(i):
        pl.semaphore_signal(
            barrier,
            inc=1,
            device_id={"dev": lax.rem(dev + i, n_dev)},
            device_id_type=pl.DeviceIdType.MESH,
        )

    each(1, n_sub, greet_sub)
    each(1, n_dev, greet_dev)

    lower = iota((BLOCK, BLOCK), 0) >= iota((BLOCK, BLOCK), 1)
    diagonal = iota((BLOCK, BLOCK), 0) == iota((BLOCK, BLOCK), 1)

    def live(g, b):
        return jnp.where(blocks_ref[sub * group + g] > b, 1.0, 0.0).astype(F32)

    def cumulative(hd, g, b):
        row = dbuf[hd, g, :, b * BLOCK : (b + 1) * BLOCK] * live(g, b)
        return jnp.sum(
            jnp.where(lower, jnp.broadcast_to(row, (BLOCK, BLOCK)), 0.0),
            axis=1,
            keepdims=True,
        )

    def state(hd, g):
        after = None
        weighted = []
        for b in reversed(range(prompt_blocks)):
            col = cumulative(hd, g, b)
            last = col[BLOCK - 1 :, :]
            tail = last - col if after is None else last - col + after
            after = last if after is None else after + last
            part = v_ref[hd, g, b * BLOCK : (b + 1) * BLOCK, :].astype(F32)
            weighted.append(part * (jnp.exp(tail) * live(g, b)))
        high, low = split(jnp.concatenate(weighted[::-1], axis=0))
        both = dot(k_ref[hd, g], jnp.concatenate([high, low], axis=1), TN)
        total = both[:, :width] + both[:, width:]
        for s in range(n_sub):
            sbuf[hd, s, g] = total[s * rows : (s + 1) * rows, :]

    def output(hd, g):
        cols = [cumulative(hd, g, b) for b in range(prompt_blocks)]
        flat = [
            jnp.sum(
                jnp.where(diagonal, jnp.broadcast_to(c, (BLOCK, BLOCK)), 0.0),
                axis=0,
                keepdims=True,
            )
            for c in cols
        ]
        for b in range(prompt_blocks):
            q = q_ref[hd, g, b * BLOCK : (b + 1) * BLOCK, :]
            total = None
            before = None
            for a in reversed(range(b + 1)):
                k = k_ref[hd, g, a * BLOCK : (a + 1) * BLOCK, :]
                v = v_ref[hd, g, a * BLOCK : (a + 1) * BLOCK, :]
                if a == b:
                    weights = jnp.where(
                        lower, jnp.exp(jnp.where(lower, cols[b] - flat[a], 0.0)), 0.0
                    )
                else:
                    gap = cols[a][BLOCK - 1 :, :] - flat[a]
                    if before is not None:
                        gap = gap + before
                    weights = jnp.exp(cols[b] + gap)
                    ending = cols[a][BLOCK - 1 :, :]
                    before = ending if before is None else before + ending
                high, low = split(dot(q, k, NT) * weights)
                term = dot(
                    jnp.concatenate([high, low], axis=1),
                    jnp.concatenate([v, v], axis=0),
                    NN,
                )
                total = term if total is None else total + term
            pbuf[hd, g, b * BLOCK : (b + 1) * BLOCK, :] = (total * live(g, b)).astype(
                BF16
            )

    def copy_a(hd, i):
        to = lax.rem(sub + i, n_sub)
        return pltpu.make_async_remote_copy(
            src_ref=sbuf.at[hd, to],
            dst_ref=mids[hd].at[pl.ds(sub * group, group)],
            send_sem=send_a.at[hd, i],
            recv_sem=recv_a.at[hd, i],
            device_id={"sub": to},
            device_id_type=pl.DeviceIdType.MESH,
        )

    def copy_b(hd, i):
        to = lax.rem(dev + i, n_dev)
        return pltpu.make_async_remote_copy(
            src_ref=bbuf.at[hd, i],
            dst_ref=rbuf.at[dev, hd],
            send_sem=send_b.at[hd, i],
            recv_sem=recv_b.at[hd, i],
            device_id={"dev": to},
            device_id_type=pl.DeviceIdType.MESH,
        )

    def copy_y(i):
        return pltpu.make_async_remote_copy(
            src_ref=ybuf.at[0],
            dst_ref=ybuf.at[i],
            send_sem=send_y.at[i],
            recv_sem=recv_y.at[i],
            device_id={"sub": lax.rem(sub + i, n_sub)},
            device_id_type=pl.DeviceIdType.MESH,
        )

    def owned(r):
        def look(n, found):
            first, second = found
            mine = dest_ref[n] == r
            return (
                jnp.where(mine, jnp.minimum(first, n), first),
                jnp.where(mine, jnp.maximum(second, n), second),
            )

        found = (jnp.int32(requests - 1), jnp.int32(0))
        if requests <= 8:
            for n in range(requests):
                found = look(n, found)
            return found
        return lax.fori_loop(0, requests, look, found)

    def decode_ahead(j, c):
        eight = iota((CHUNK, CHUNK), 0) == iota((CHUNK, CHUNK), 1)
        n = steps * CHUNK
        pieces = []
        total = jnp.zeros((1, CHUNK), F32)
        for s in range(steps):
            total = total + dd_ref[j, s : s + 1, c * CHUNK : (c + 1) * CHUNK]
            pieces.append(
                jnp.sum(
                    jnp.where(eight, jnp.broadcast_to(total, (CHUNK, CHUNK)), 0.0),
                    axis=1,
                    keepdims=True,
                )
            )
        col = jnp.concatenate(pieces, axis=0)
        square_row, square_col = iota((n, n), 0), iota((n, n), 1)
        row = jnp.sum(
            jnp.where(square_row == square_col, jnp.broadcast_to(col, (n, n)), 0.0),
            axis=0,
            keepdims=True,
        )
        seen = ((square_row & (CHUNK - 1)) == (square_col & (CHUNK - 1))) & (
            square_row >= square_col
        )
        weights = jnp.where(seen, jnp.exp(jnp.where(seen, col - row, 0.0)), 0.0)
        spread = (
            iota((rows, lanes), 0) == lax.rem(iota((rows, lanes), 1), rows)
        ).astype(BF16)
        own = iota((CHUNK, lanes), 0) == lax.div(iota((CHUNK, lanes), 1), rows)

        def diagonal_blocks(ref):
            return jnp.concatenate(
                [
                    jnp.where(
                        own,
                        dot(ref[j, s, c * CHUNK : (c + 1) * CHUNK, :], spread, NN),
                        0.0,
                    )
                    for s in range(steps)
                ],
                axis=0,
            )

        qb = diagonal_blocks(qd_ref).astype(BF16)
        kb = diagonal_blocks(kd_ref)
        vb = jnp.concatenate(
            [
                vd_ref[j, s, c * CHUNK : (c + 1) * CHUNK, :].astype(F32)
                for s in range(steps)
            ],
            axis=0,
        )
        mixed = dot(qb, kb.astype(BF16), NT) * weights
        ybuf[0, c, j] = dot(mixed, vb, NN, HIGHEST)
        tail = jnp.exp(jnp.concatenate([pieces[-1]] * steps, axis=0) - col)
        update = dot(kb * tail, vb, TN, HIGHEST)
        for h in range(CHUNK):
            fsbuf[j, c * CHUNK + h] = update[h * rows : (h + 1) * rows, :]
        qbuf[c, j] = qb
        ebuf[c, j] = jnp.broadcast_to(jnp.exp(col), (n, width))

    def decode(j, c):
        per = CHUNK // heads
        last = (steps - 1) * CHUNK
        parts = [
            rbuf[c * per + h // heads, h % heads, j] for h in range(CHUNK)
        ]
        high, low = split(jnp.concatenate(parts, axis=0))
        both = dot(qbuf[c, j], jnp.concatenate([high, low], axis=1), NN)
        ybuf[0, c, j] = (both[:, :width] + both[:, width:]) * ebuf[c, j] + ybuf[0, c, j]
        for h in range(CHUNK):
            fsbuf[j, c * CHUNK + h] = (
                parts[h] * ebuf[c, j, last + h : last + h + 1, :]
                + fsbuf[j, c * CHUNK + h]
            )

    for load in loads[:3]:
        load.wait()
    for hd in range(heads):
        for g in range(group):
            dbuf[hd, g] = d_ref[hd, g : g + 1, :]
        each(0, group, functools.partial(state, hd))
        if hd == 0:
            pl.semaphore_wait(barrier, n_sub - 1 + n_dev - 1)
        each(1, n_sub, lambda i: copy_a(hd, i).start())
        mids[hd][pl.ds(sub * group, group)] = sbuf[hd, sub]
    for load in loads[3:]:
        load.wait()

    def save(hd):
        return pltpu.make_async_copy(pbuf.at[hd], out_hbm.at[hd], saved.at[hd])

    for hd in range(heads):
        each(1, n_sub, lambda i: copy_a(hd, i).wait_recv())

        def pass_on(i):
            first, second = owned(lax.rem(dev + i, n_dev))
            bbuf[hd, i, 0] = mids[hd][first]
            bbuf[hd, i, 1] = mids[hd][second]
            copy_b(hd, i).start()

        each(1, n_dev, pass_on)
        first, second = owned(dev)
        rbuf[dev, hd, 0] = mids[hd][first]
        rbuf[dev, hd, 1] = mids[hd][second]
        if hd + 1 < heads:
            each(0, group, functools.partial(output, hd))
            save(hd).start()

    for c in range(chunks):
        for j in range(slots):
            decode_ahead(j, c)
    each(0, group, functools.partial(output, heads - 1))
    save(heads - 1).start()

    for hd in range(heads):
        each(1, n_dev, lambda i: copy_b(hd, i).wait_recv())
    for c in range(chunks):
        for j in range(slots):
            decode(j, c)
    each(1, n_sub, lambda i: copy_y(i).start())
    final = pltpu.make_async_copy(fsbuf, fin_hbm, saved.at[heads])
    final.start()
    share = all_heads // n_sub
    gates = [
        jax.nn.sigmoid(gate_ref[j].astype(F32)) * gain_ref[...] for j in range(slots)
    ]
    for hd in range(heads):
        each(1, n_sub, lambda i: copy_a(hd, i).wait_send())
        each(1, n_dev, lambda i: copy_b(hd, i).wait_send())
        save(hd).wait()
    each(1, n_sub, lambda i: copy_y(i).wait_recv())
    for j in range(slots):
        square = jnp.zeros((steps, width), F32)
        for c in range(chunks):
            y = ybuf[0, c, j]
            for i in range(1, n_sub):
                y = y + ybuf[i, c, j]
            for s in range(steps):
                ysum[j, s, c * CHUNK : (c + 1) * CHUNK, :] = y[
                    s * CHUNK : (s + 1) * CHUNK, :
                ]
            square = square + jnp.sum((y * y).reshape(steps, CHUNK, width), axis=1)
        mean = jnp.sum(square, axis=1, keepdims=True) / (all_heads * width)
        inverse = lax.rsqrt(mean + EPSILON)
        for h in range(share):
            y = jnp.concatenate(
                [ysum[j, s, pl.ds(sub * share + h, 1), :] for s in range(steps)], axis=0
            )
            gate = gates[j][:, h * width : (h + 1) * width]
            dec_ref[j, :, h * width : (h + 1) * width] = (y * inverse * gate).astype(
                BF16
            )
    each(1, n_sub, lambda i: copy_y(i).wait_send())
    final.wait()


def finish(*refs):
    sems = refs[-1]
    half = (len(refs) - 1) // 2
    saves = [
        pltpu.make_async_copy(refs[i], refs[half + i], sems.at[i]) for i in range(half)
    ]
    for save in saves:
        save.start()
    for save in saves:
        save.wait()


def body(n_dev, n_sub, *args):
    q, k, v, d, blocks, dest, qd, kd, vd, dd, gate, gain = args
    heads, group, length, width = q.shape
    slots, steps, rows, all_heads = qd.shape
    requests = dest.shape[0]
    chunks = all_heads // CHUNK
    vmem = pl.BlockSpec(memory_space=pltpu.VMEM)
    smem = pl.BlockSpec(memory_space=pltpu.SMEM)
    hbm = pl.BlockSpec(memory_space=pltpu.HBM)
    dma = pltpu.SemaphoreType.DMA
    turned = (slots, steps, all_heads, rows)
    state = jax.ShapeDtypeStruct((slots, all_heads, rows, width), F32)
    shapes = (
        jax.ShapeDtypeStruct(q.shape, BF16),
        jax.ShapeDtypeStruct(gate.shape, BF16),
        state,
    )
    made = pl.pallas_call(
        functools.partial(kernel, n_dev, n_sub),
        out_shape=shapes,
        in_specs=[hbm] * 4 + [smem] * 2 + [hbm] * 6,
        out_specs=(hbm, vmem, hbm),
        scratch_shapes=[
            pltpu.VMEM(q.shape, BF16),
            pltpu.VMEM(state.shape, F32),
            pltpu.VMEM((n_sub, chunks, slots, steps * CHUNK, width), F32),
            pltpu.VMEM((slots, steps, all_heads, width), F32),
            pltpu.VMEM(gate.shape, BF16),
            pltpu.VMEM((1, gain.shape[0]), F32),
            pltpu.VMEM(q.shape, BF16),
            pltpu.VMEM(q.shape, BF16),
            pltpu.VMEM(q.shape, BF16),
            pltpu.VMEM(d.shape, F32),
            pltpu.VMEM(turned, BF16),
            pltpu.VMEM(turned, BF16),
            pltpu.VMEM(vd.shape, BF16),
            pltpu.VMEM(dd.shape, F32),
            pltpu.VMEM((heads, n_sub, group, rows, width), F32),
            pltpu.VMEM((heads, n_dev, slots, rows, width), F32),
            pltpu.VMEM((n_dev, heads, slots, rows, width), F32),
            pltpu.VMEM((heads, group, 1, length), F32),
            pltpu.VMEM((chunks, slots, steps * CHUNK, CHUNK * rows), BF16),
            pltpu.VMEM((chunks, slots, steps * CHUNK, width), F32),
            dma((heads, n_sub)),
            dma((heads, n_sub)),
            dma((heads, n_dev)),
            dma((heads, n_dev)),
            dma((n_sub,)),
            dma((n_sub,)),
            dma((10,)),
            dma((heads + 1,)),
        ]
        + [pltpu.VMEM((requests, rows, width), F32)] * heads,
        compiler_params=pltpu.CompilerParams(
            collective_id=0, has_side_effects=True, vmem_limit_bytes=64 * 2**20
        ),
    )(
        q,
        k,
        v,
        d,
        blocks,
        dest,
        jnp.swapaxes(qd, 2, 3),
        jnp.swapaxes(kd, 2, 3),
        vd,
        dd,
        gate,
        gain.reshape(1, -1),
    )
    return pl.pallas_call(
        finish,
        out_shape=shapes,
        in_specs=[hbm] * 3,
        out_specs=(hbm,) * 3,
        scratch_shapes=[dma((3,))],
        compiler_params=pltpu.CompilerParams(vmem_limit_bytes=64 * 2**20),
    )(*made)


def solution(mesh):
    placed = (
        P("dev", ("groups", "sub"), None, None),
        P("dev", ("groups", "sub"), None, None),
        P("dev", ("groups", "sub"), None, None),
        P("dev", ("groups", "sub"), None),
        P("groups"),
        P("groups"),
        P(("groups", "dev"), None, "sub", None),
        P(("groups", "dev"), None, "sub", None),
        P(("groups", "dev"), None, None, None),
        P(("groups", "dev"), None, None),
        P(("groups", "dev"), None, "sub"),
        P("sub"),
    )
    return jax.shard_map(
        functools.partial(body, mesh.shape["dev"], mesh.shape["sub"]),
        mesh=mesh,
        in_specs=placed,
        out_specs=(
            P("dev", ("groups", "sub"), None, None),
            P(("groups", "dev"), None, "sub"),
            P(("groups", "dev"), None, "sub", None),
        ),
        check_vma=False,
    )
```

```python
import functools
import math

import jax
import jax.numpy as jnp
from jax import lax
from jax.experimental import pallas as pl
from jax.experimental.pallas import tpu as pltpu
from jax.sharding import PartitionSpec as P

BLOCK = 128
EPSILON = 1e-06
HIGHEST = lax.Precision.HIGHEST
F32 = jnp.float32
BF16 = jnp.bfloat16
CHUNK = 8


def each(low, high, step):
    if high - low <= 8:
        for i in range(low, high):
            step(i)
    else:

        def turn(i, carry):
            step(i)
            return carry

        lax.fori_loop(low, high, turn, 0)


def dot(a, b, contract, precision=None):
    return lax.dot_general(
        a, b, (contract, ((), ())), precision=precision, preferred_element_type=F32
    )


NN = ((1,), (0,))
NT = ((1,), (1,))
TN = ((0,), (0,))


def split(x):
    high = x.astype(BF16)
    return high, (x - high.astype(F32)).astype(BF16)


def iota(shape, dimension):
    return lax.broadcasted_iota(jnp.int32, shape, dimension)


def kernel(
    n_dev,
    n_sub,
    q_hbm,
    k_hbm,
    v_hbm,
    d_hbm,
    blocks_ref,
    dest_ref,
    qd_hbm,
    kd_hbm,
    vd_hbm,
    dd_hbm,
    gate_hbm,
    gain_hbm,
    pbuf,
    fsbuf,
    ybuf,
    scale_ref,
    q_ref,
    k_ref,
    v_ref,
    d_ref,
    qd_ref,
    kd_ref,
    vd_ref,
    dd_ref,
    gate_ref,
    gain_ref,
    sbuf,
    bbuf,
    rbuf,
    dbuf,
    qbuf,
    ebuf,
    send_a,
    recv_a,
    send_b,
    recv_b,
    send_y,
    recv_y,
    local,
    *mids,
):
    heads, group, length, width = q_ref.shape
    prompt_blocks = length // BLOCK
    slots, steps, all_heads, rows = qd_ref.shape
    requests = dest_ref.shape[0]
    chunks = all_heads // CHUNK
    lanes = CHUNK * rows
    sub = lax.axis_index("sub")
    dev = lax.axis_index("dev")

    loads = [
        pltpu.make_async_copy(source, target, local.at[i])
        for i, (source, target) in enumerate(
            (
                (d_hbm, d_ref),
                (v_hbm, v_ref),
                (k_hbm, k_ref),
                (q_hbm, q_ref),
                (dd_hbm, dd_ref),
                (kd_hbm, kd_ref),
                (qd_hbm, qd_ref),
                (vd_hbm, vd_ref),
                (gate_hbm, gate_ref),
                (gain_hbm, gain_ref),
            )
        )
    ]
    for load in loads:
        load.start()
    barrier = pltpu.get_barrier_semaphore()

    def greet_sub(i):
        pl.semaphore_signal(
            barrier,
            inc=1,
            device_id={"sub": lax.rem(sub + i, n_sub)},
            device_id_type=pl.DeviceIdType.MESH,
        )

    def greet_dev(i):
        pl.semaphore_signal(
            barrier,
            inc=1,
            device_id={"dev": lax.rem(dev + i, n_dev)},
            device_id_type=pl.DeviceIdType.MESH,
        )

    each(1, n_sub, greet_sub)
    each(1, n_dev, greet_dev)

    lower = iota((BLOCK, BLOCK), 0) >= iota((BLOCK, BLOCK), 1)
    diagonal = iota((BLOCK, BLOCK), 0) == iota((BLOCK, BLOCK), 1)

    def live(g, b):
        return jnp.where(blocks_ref[sub * group + g] > b, 1.0, 0.0).astype(F32)

    def cumulative(hd, g, b):
        row = dbuf[hd, g, :, b * BLOCK : (b + 1) * BLOCK] * live(g, b)
        return jnp.sum(
            jnp.where(lower, jnp.broadcast_to(row, (BLOCK, BLOCK)), 0.0),
            axis=1,
            keepdims=True,
        )

    def state(hd, g):
        after = None
        weighted = []
        for b in reversed(range(prompt_blocks)):
            col = cumulative(hd, g, b)
            last = col[BLOCK - 1 :, :]
            tail = last - col if after is None else last - col + after
            after = last if after is None else after + last
            part = v_ref[hd, g, b * BLOCK : (b + 1) * BLOCK, :].astype(F32)
            weighted.append(part * (jnp.exp(tail) * live(g, b)))
        high, low = split(jnp.concatenate(weighted[::-1], axis=0))
        both = dot(k_ref[hd, g], jnp.concatenate([high, low], axis=1), TN)
        total = both[:, :width] + both[:, width:]
        for s in range(n_sub):
            sbuf[hd, s, g] = total[s * rows : (s + 1) * rows, :]

    def output(hd, g):
        cols = [cumulative(hd, g, b) for b in range(prompt_blocks)]
        flat = [
            jnp.sum(
                jnp.where(diagonal, jnp.broadcast_to(c, (BLOCK, BLOCK)), 0.0),
                axis=0,
                keepdims=True,
            )
            for c in cols
        ]
        for b in range(prompt_blocks):
            q = q_ref[hd, g, b * BLOCK : (b + 1) * BLOCK, :]
            total = None
            before = None
            for a in reversed(range(b + 1)):
                k = k_ref[hd, g, a * BLOCK : (a + 1) * BLOCK, :]
                v = v_ref[hd, g, a * BLOCK : (a + 1) * BLOCK, :]
                if a == b:
                    weights = jnp.where(
                        lower, jnp.exp(jnp.where(lower, cols[b] - flat[a], 0.0)), 0.0
                    )
                else:
                    gap = cols[a][BLOCK - 1 :, :] - flat[a]
                    if before is not None:
                        gap = gap + before
                    weights = jnp.exp(cols[b] + gap)
                    ending = cols[a][BLOCK - 1 :, :]
                    before = ending if before is None else before + ending
                high, low = split(dot(q, k, NT) * weights)
                term = dot(
                    jnp.concatenate([high, low], axis=1),
                    jnp.concatenate([v, v], axis=0),
                    NN,
                )
                total = term if total is None else total + term
            pbuf[hd, g, b * BLOCK : (b + 1) * BLOCK, :] = (total * live(g, b)).astype(
                BF16
            )

    def copy_a(hd, i):
        to = lax.rem(sub + i, n_sub)
        return pltpu.make_async_remote_copy(
            src_ref=sbuf.at[hd, to],
            dst_ref=mids[hd].at[pl.ds(sub * group, group)],
            send_sem=send_a.at[hd, i],
            recv_sem=recv_a.at[hd, i],
            device_id={"sub": to},
            device_id_type=pl.DeviceIdType.MESH,
        )

    def copy_b(hd, i):
        to = lax.rem(dev + i, n_dev)
        return pltpu.make_async_remote_copy(
            src_ref=bbuf.at[hd, i],
            dst_ref=rbuf.at[dev, hd],
            send_sem=send_b.at[hd, i],
            recv_sem=recv_b.at[hd, i],
            device_id={"dev": to},
            device_id_type=pl.DeviceIdType.MESH,
        )

    def copy_y(i):
        return pltpu.make_async_remote_copy(
            src_ref=ybuf.at[0],
            dst_ref=ybuf.at[i],
            send_sem=send_y.at[i],
            recv_sem=recv_y.at[i],
            device_id={"sub": lax.rem(sub + i, n_sub)},
            device_id_type=pl.DeviceIdType.MESH,
        )

    def owned(r):
        def look(n, found):
            first, second = found
            mine = dest_ref[n] == r
            return (
                jnp.where(mine, jnp.minimum(first, n), first),
                jnp.where(mine, jnp.maximum(second, n), second),
            )

        found = (jnp.int32(requests - 1), jnp.int32(0))
        if requests <= 8:
            for n in range(requests):
                found = look(n, found)
            return found
        return lax.fori_loop(0, requests, look, found)

    def decode_ahead(j, c):
        eight = iota((CHUNK, CHUNK), 0) == iota((CHUNK, CHUNK), 1)
        n = steps * CHUNK
        pieces = []
        total = jnp.zeros((1, CHUNK), F32)
        for s in range(steps):
            total = total + dd_ref[j, s : s + 1, c * CHUNK : (c + 1) * CHUNK]
            pieces.append(
                jnp.sum(
                    jnp.where(eight, jnp.broadcast_to(total, (CHUNK, CHUNK)), 0.0),
                    axis=1,
                    keepdims=True,
                )
            )
        col = jnp.concatenate(pieces, axis=0)
        square_row, square_col = iota((n, n), 0), iota((n, n), 1)
        row = jnp.sum(
            jnp.where(square_row == square_col, jnp.broadcast_to(col, (n, n)), 0.0),
            axis=0,
            keepdims=True,
        )
        seen = ((square_row & (CHUNK - 1)) == (square_col & (CHUNK - 1))) & (
            square_row >= square_col
        )
        weights = jnp.where(seen, jnp.exp(jnp.where(seen, col - row, 0.0)), 0.0)
        spread = (
            iota((rows, lanes), 0) == lax.rem(iota((rows, lanes), 1), rows)
        ).astype(BF16)
        own = iota((CHUNK, lanes), 0) == lax.div(iota((CHUNK, lanes), 1), rows)

        def diagonal_blocks(ref):
            return jnp.concatenate(
                [
                    jnp.where(
                        own,
                        dot(ref[j, s, c * CHUNK : (c + 1) * CHUNK, :], spread, NN),
                        0.0,
                    )
                    for s in range(steps)
                ],
                axis=0,
            )

        qb = diagonal_blocks(qd_ref).astype(BF16)
        kb = diagonal_blocks(kd_ref)
        vb = jnp.concatenate(
            [
                vd_ref[j, s, c * CHUNK : (c + 1) * CHUNK, :].astype(F32)
                for s in range(steps)
            ],
            axis=0,
        )
        mixed = dot(qb, kb.astype(BF16), NT) * weights
        ybuf[0, c, j] = dot(mixed, vb, NN, HIGHEST)
        tail = jnp.exp(jnp.concatenate([pieces[-1]] * steps, axis=0) - col)
        update = dot(kb * tail, vb, TN, HIGHEST)
        for h in range(CHUNK):
            fsbuf[j, c * CHUNK + h] = update[h * rows : (h + 1) * rows, :]
        qbuf[c, j] = qb
        ebuf[c, j] = jnp.broadcast_to(jnp.exp(col), (n, width))

    def decode(j, c):
        per = CHUNK // heads
        last = (steps - 1) * CHUNK
        parts = [
            rbuf[c * per + h // heads, h % heads, j] for h in range(CHUNK)
        ]
        high, low = split(jnp.concatenate(parts, axis=0))
        both = dot(qbuf[c, j], jnp.concatenate([high, low], axis=1), NN)
        ybuf[0, c, j] = (both[:, :width] + both[:, width:]) * ebuf[c, j] + ybuf[0, c, j]
        for h in range(CHUNK):
            fsbuf[j, c * CHUNK + h] = (
                parts[h] * ebuf[c, j, last + h : last + h + 1, :]
                + fsbuf[j, c * CHUNK + h]
            )

    for load in loads[:3]:
        load.wait()
    for hd in range(heads):
        for g in range(group):
            dbuf[hd, g] = d_ref[hd, g : g + 1, :]
        each(0, group, functools.partial(state, hd))
        if hd == 0:
            pl.semaphore_wait(barrier, n_sub - 1 + n_dev - 1)
        each(1, n_sub, lambda i: copy_a(hd, i).start())
        mids[hd][pl.ds(sub * group, group)] = sbuf[hd, sub]
    for load in loads[3:]:
        load.wait()

    for hd in range(heads):
        each(1, n_sub, lambda i: copy_a(hd, i).wait_recv())

        def pass_on(i):
            first, second = owned(lax.rem(dev + i, n_dev))
            bbuf[hd, i, 0] = mids[hd][first]
            bbuf[hd, i, 1] = mids[hd][second]
            copy_b(hd, i).start()

        each(1, n_dev, pass_on)
        first, second = owned(dev)
        rbuf[dev, hd, 0] = mids[hd][first]
        rbuf[dev, hd, 1] = mids[hd][second]
        if hd + 1 < heads:
            each(0, group, functools.partial(output, hd))

    for c in range(chunks):
        for j in range(slots):
            decode_ahead(j, c)
    each(0, group, functools.partial(output, heads - 1))
    for j in range(slots):
        scale_ref[j] = jax.nn.sigmoid(gate_ref[j].astype(F32)) * gain_ref[...]

    for hd in range(heads):
        each(1, n_dev, lambda i: copy_b(hd, i).wait_recv())
    for c in range(chunks):
        for j in range(slots):
            decode(j, c)
    each(1, n_sub, lambda i: copy_y(i).start())
    for hd in range(heads):
        each(1, n_sub, lambda i: copy_a(hd, i).wait_send())
        each(1, n_dev, lambda i: copy_b(hd, i).wait_send())
    each(1, n_sub, lambda i: copy_y(i).wait())


def finish(
    n_sub, out_ref, fin_ref, y_ref, scale_ref, out_hbm, dec_ref, fin_hbm, ysum, sems
):
    saves = [
        pltpu.make_async_copy(out_ref, out_hbm, sems.at[0]),
        pltpu.make_async_copy(fin_ref, fin_hbm, sems.at[1]),
    ]
    for save in saves:
        save.start()
    _, chunks, slots, _, width = y_ref.shape
    _, steps, all_heads, _ = ysum.shape
    sub = lax.axis_index("sub")
    share = all_heads // n_sub
    for j in range(slots):
        square = jnp.zeros((steps, width), F32)
        for c in range(chunks):
            y = y_ref[0, c, j]
            for i in range(1, n_sub):
                y = y + y_ref[i, c, j]
            for s in range(steps):
                ysum[j, s, c * CHUNK : (c + 1) * CHUNK, :] = y[
                    s * CHUNK : (s + 1) * CHUNK, :
                ]
            square = square + jnp.sum((y * y).reshape(steps, CHUNK, width), axis=1)
        mean = jnp.sum(square, axis=1, keepdims=True) / (all_heads * width)
        inverse = lax.rsqrt(mean + EPSILON)
        gates = scale_ref[j]
        for h in range(share):
            y = jnp.concatenate(
                [ysum[j, s, pl.ds(sub * share + h, 1), :] for s in range(steps)], axis=0
            )
            gate = gates[:, h * width : (h + 1) * width]
            dec_ref[j, :, h * width : (h + 1) * width] = (y * inverse * gate).astype(
                BF16
            )
    for save in saves:
        save.wait()


def body(n_dev, n_sub, *args):
    q, k, v, d, blocks, dest, qd, kd, vd, dd, gate, gain = args
    heads, group, length, width = q.shape
    slots, steps, rows, all_heads = qd.shape
    requests = dest.shape[0]
    chunks = all_heads // CHUNK
    vmem = pl.BlockSpec(memory_space=pltpu.VMEM)
    smem = pl.BlockSpec(memory_space=pltpu.SMEM)
    hbm = pl.BlockSpec(memory_space=pltpu.HBM)
    dma = pltpu.SemaphoreType.DMA
    turned = (slots, steps, all_heads, rows)
    state = jax.ShapeDtypeStruct((slots, all_heads, rows, width), F32)
    parts = (n_sub, chunks, slots, steps * CHUNK, width)
    kept = 2 * math.prod(q.shape) + 4 * (math.prod(state.shape) + math.prod(parts))
    limit = 62 * 2**20 - kept
    made = pl.pallas_call(
        functools.partial(kernel, n_dev, n_sub),
        out_shape=(
            pltpu.VMEM(q.shape, BF16),
            pltpu.VMEM(state.shape, F32),
            pltpu.VMEM(parts, F32),
            pltpu.VMEM((slots, steps, gain.shape[0]), F32),
        ),
        in_specs=[hbm] * 4 + [smem] * 2 + [hbm] * 6,
        out_specs=(vmem, vmem, vmem, vmem),
        scratch_shapes=[
            pltpu.VMEM(q.shape, BF16),
            pltpu.VMEM(q.shape, BF16),
            pltpu.VMEM(q.shape, BF16),
            pltpu.VMEM(d.shape, F32),
            pltpu.VMEM(turned, BF16),
            pltpu.VMEM(turned, BF16),
            pltpu.VMEM(vd.shape, BF16),
            pltpu.VMEM(dd.shape, F32),
            pltpu.VMEM(gate.shape, BF16),
            pltpu.VMEM((1, gain.shape[0]), F32),
            pltpu.VMEM((heads, n_sub, group, rows, width), F32),
            pltpu.VMEM((heads, n_dev, slots, rows, width), F32),
            pltpu.VMEM((n_dev, heads, slots, rows, width), F32),
            pltpu.VMEM((heads, group, 1, length), F32),
            pltpu.VMEM((chunks, slots, steps * CHUNK, CHUNK * rows), BF16),
            pltpu.VMEM((chunks, slots, steps * CHUNK, width), F32),
            dma((heads, n_sub)),
            dma((heads, n_sub)),
            dma((heads, n_dev)),
            dma((heads, n_dev)),
            dma((n_sub,)),
            dma((n_sub,)),
            dma((10,)),
        ]
        + [pltpu.VMEM((requests, rows, width), F32)] * heads,
        compiler_params=pltpu.CompilerParams(
            collective_id=0, has_side_effects=True, vmem_limit_bytes=limit
        ),
    )(
        q,
        k,
        v,
        d,
        blocks,
        dest,
        jnp.swapaxes(qd, 2, 3),
        jnp.swapaxes(kd, 2, 3),
        vd,
        dd,
        gate,
        gain.reshape(1, -1),
    )
    out, dec, fin = pl.pallas_call(
        functools.partial(finish, n_sub),
        out_shape=(
            jax.ShapeDtypeStruct(q.shape, BF16),
            jax.ShapeDtypeStruct(gate.shape, BF16),
            state,
        ),
        in_specs=[vmem] * 4,
        out_specs=(hbm, vmem, hbm),
        scratch_shapes=[pltpu.VMEM((slots, steps, all_heads, width), F32), dma((2,))],
        compiler_params=pltpu.CompilerParams(vmem_limit_bytes=16 * 2**20),
    )(*made)
    return out, dec, fin


def solution(mesh):
    placed = (
        P("dev", ("groups", "sub"), None, None),
        P("dev", ("groups", "sub"), None, None),
        P("dev", ("groups", "sub"), None, None),
        P("dev", ("groups", "sub"), None),
        P("groups"),
        P("groups"),
        P(("groups", "dev"), None, "sub", None),
        P(("groups", "dev"), None, "sub", None),
        P(("groups", "dev"), None, None, None),
        P(("groups", "dev"), None, None),
        P(("groups", "dev"), None, "sub"),
        P("sub"),
    )
    return jax.shard_map(
        functools.partial(body, mesh.shape["dev"], mesh.shape["sub"]),
        mesh=mesh,
        in_specs=placed,
        out_specs=(
            P("dev", ("groups", "sub"), None, None),
            P(("groups", "dev"), None, "sub"),
            P(("groups", "dev"), None, "sub", None),
        ),
        check_vma=False,
    )
```
